32 devices in a mesh: row: 4 (over z), col: 8 (over y, x, core).
Axes of the slice: x: 2, y: 2, z: 4, core: 2. Of those that a mesh axis runs over, the one named last changes fastest.
Arguments:
- amplitudes: float32 [1024, 131072], P('col', 'row'), may hold values from -6 to 6
- integrals: float32 [131072, 3072], P(('row', 'col')), may hold values from -0.03125 to 0.03125
Outputs:
- ladder: float32 [1024, 3072], P('col', 'row')
The draws below stay inside these ranges and needn't reach their ends.
All inputs are finite; a program needn't handle non-finite values.
Results may differ from the reference program's by a relative error of at most 0.00011.
Values sent between devices are 32-bit elements; how exact they have to be, the bound alone decides.
A program may use at most 192 MiB of HBM per device.

```python
import jax
import jax.numpy as jnp
from jax import lax

NAB = 3072
NOP = 1024
CD = 131072


def with_spikes(array, stream_key, source, target, parts, factor):
    owner, partner = [(jnp.arange(array.shape[axis_at]) // (array.shape[axis_at] // parts)).reshape([-1 if axis == axis_at else 1 for axis in range(array.ndim)]) for axis_at in (source, target)]
    chosen = jax.random.permutation(stream_key, parts)[partner]
    strong = (owner == chosen) | (owner == (partner + parts // 2) % parts)
    return jnp.where(strong, factor * array, array)


def block_scale(key, extent, pieces, low, high):
    def one(position, shards_of):
        steps = jax.random.uniform(jax.random.fold_in(jax.random.fold_in(key, 6), position), (shards_of,), jnp.float32, low / len(pieces), high / len(pieces))
        return jnp.repeat(jnp.exp(steps), extent[position] // shards_of).reshape((-1,) + (1,) * (len(extent) - position - 1))

    loudness = one(*pieces[0])
    for cut in pieces[1:]:
        loudness = loudness * one(*cut)
    return loudness


def scatter_about(rng, dims, spread, reach, cuts=(), kind=jnp.bfloat16):
    gain = block_scale(rng, dims, cuts, -0.22, 0.18) if cuts else 1.0
    entries = jax.random.normal(rng, dims, jnp.float32) * spread * gain
    return jnp.minimum(jnp.maximum(entries, -reach), reach).astype(kind)


def bell_draw_with(rng, shape, width, bound, pieces, heavy, held_as=jnp.bfloat16):
    values = width * jax.random.normal(rng, shape, jnp.float32)
    if pieces:
        values = values * block_scale(rng, shape, pieces, -0.22, 0.18)
    return jnp.clip(with_spikes(values, jax.random.fold_in(rng, 3), *heavy), -bound, bound).astype(held_as)


def setup_inputs(seed: int = 0) -> dict:
    streams_of = jax.random.split(jax.random.key(seed), 3)
    return {
        "amplitudes": scatter_about(streams_of[0], (NOP, CD), 1.0, 6.0, ((0, 8), (1, 4)), jnp.float32),
        "integrals": bell_draw_with(streams_of[1], (CD, NAB), CD ** -0.5, 0.03125, ((0, 32),), (0, 1, 32, 2.75), jnp.float32),
    }


def reference(amplitudes, integrals):
    product = jnp.dot(amplitudes, integrals, precision=lax.Precision.HIGHEST, preferred_element_type=jnp.float32)
    return 0.5 * product
```

```python
import functools

import jax
import jax.numpy as jnp
from jax import lax
from jax.experimental import pallas as pl
from jax.experimental.pallas import tpu as pltpu
from jax.sharding import PartitionSpec as P

MESH = pl.DeviceIdType.MESH
BF16, F32 = jnp.bfloat16, jnp.float32
SLOTS = 3
CHUNKS = 4


def kernel(
    rows, cols, m, chunks, depth, tn, kt,
    a, b, out,
    recv, xhi, xlo, bbuf, acc, part, pair_in, z_in, plane, plane_in,
    own_sem, a_send, a_recv, b_sem, p_send, p_recv, z_send, z_recv, q_send, q_recv,
):
    r, c = lax.axis_index("row"), lax.axis_index("col")
    chips = cols // 2
    core, chip = lax.rem(c, 2), lax.div(c, 2)
    sibling = c + 1 - 2 * core
    half = chips * m
    slab = out.shape[1]
    per = slab // tn
    tiles = rows * per

    def place(col):
        return pl.multiple_of((lax.rem(col, 2) * chips + lax.div(col, 2)) * m, 8)

    def own_copy(s):
        return pltpu.make_async_copy(
            a.at[pl.ds(pl.multiple_of(s * m, 8), m), pl.ds(pl.multiple_of(c * depth, 128), depth)],
            recv.at[s, pl.ds(place(c), m)],
            own_sem.at[s],
        )

    def a_copy(s, k, slot_of):
        peer = lax.rem(c + k, cols)
        return pltpu.make_async_remote_copy(
            src_ref=a.at[
                pl.ds(pl.multiple_of(s * m, 8), m), pl.ds(pl.multiple_of(peer * depth, 128), depth)
            ],
            dst_ref=recv.at[s, pl.ds(place(slot_of), m)],
            send_sem=a_send.at[s, k - 1],
            recv_sem=a_recv.at[s, k - 1],
            device_id={"col": peer},
            device_id_type=MESH,
        )

    def b_copy(t):
        j = lax.rem(t, tiles)
        rr = lax.rem(r + 1 + lax.div(j, per), rows)
        col = rr * slab + lax.rem(j, per) * tn
        return pltpu.make_async_copy(
            b.at[:, pl.ds(pl.multiple_of(col, 128), tn)],
            bbuf.at[lax.rem(t, SLOTS)],
            b_sem.at[lax.rem(t, SLOTS)],
        )

    def pair_copy(s, jr):
        rr = lax.rem(r + 1 + jr, rows)
        return pltpu.make_async_remote_copy(
            src_ref=part.at[lax.rem(s, 2), 1 - core, rr],
            dst_ref=pair_in.at[s, jr],
            send_sem=p_send.at[s, jr],
            recv_sem=p_recv.at[s, jr],
            device_id={"col": sibling},
            device_id_type=MESH,
        )

    def z_copy(s, jr):
        rr = lax.rem(r + 1 + jr, rows)
        return pltpu.make_async_remote_copy(
            src_ref=part.at[lax.rem(s, 2), core, rr],
            dst_ref=z_in.at[s, jr],
            send_sem=z_send.at[s, jr],
            recv_sem=z_recv.at[s, jr],
            device_id={"row": rr},
            device_id_type=MESH,
        )

    def plane_copy(s, k):
        there = lax.rem(chip + k, chips)
        return pltpu.make_async_remote_copy(
            src_ref=plane.at[s, pl.ds(pl.multiple_of(there * m, 8), m)],
            dst_ref=plane_in.at[s, k - 1],
            send_sem=q_send.at[s, k - 1],
            recv_sem=q_recv.at[s, k - 1],
            device_id={"col": 2 * there + core},
            device_id_type=MESH,
        )

    def pair_finish(s, jr):
        rr = lax.rem(r + 1 + jr, rows)
        copy = pair_copy(s, jr)
        copy.wait_recv()
        copy.wait_send()
        now = lax.rem(s, 2)
        part[now, core, rr] = part[now, core, rr] + pair_in[s, jr]

    def z_finish(s):
        @pl.loop(0, rows - 1)
        def _(k):
            copy = z_copy(s, k)
            copy.wait_recv()
            copy.wait_send()

        total = part[lax.rem(s, 2), core, r]
        for k in range(rows - 1):
            total = total + z_in[s, k]
        plane[s] = total

        @pl.loop(1, chips)
        def _(k):
            plane_copy(s, k).start()

    def plane_finish(s):
        @pl.loop(1, chips)
        def _(k):
            copy = plane_copy(s, k)
            copy.wait_recv()
            copy.wait_send()

        total = plane[s, pl.ds(pl.multiple_of(chip * m, 8), m)]
        for k in range(chips - 1):
            total = total + plane_in[s, k]
        out[pl.ds(pl.multiple_of(s * m, 8), m), :] = 0.5 * total

    def tile(s, jr, jt):
        rr = lax.rem(r + 1 + jr, rows)
        t = s * tiles + jr * per + jt
        b_copy(t).wait()

        @pl.when(t + SLOTS - 1 < chunks * tiles)
        def _():
            b_copy(t + SLOTS - 1).start()

        slot = lax.rem(t, SLOTS)
        acc[...] = jnp.zeros_like(acc)

        @pl.loop(0, depth // kt)
        def _(kk):
            at = pl.ds(pl.multiple_of(kk * kt, 128), kt)
            block = bbuf[slot, at, :]
            bh = block.astype(BF16)
            bl = (block - bh.astype(F32)).astype(BF16)
            xh, xl = xhi[:, at], xlo[:, at]
            acc[...] += (
                jnp.dot(xh, bh, preferred_element_type=F32)
                + jnp.dot(xl, bh, preferred_element_type=F32)
                + jnp.dot(xh, bl, preferred_element_type=F32)
            )

        now = lax.rem(s, 2)
        at = pl.ds(pl.multiple_of(jt * tn, 128), tn)
        part[now, 0, rr, :, at] = acc[:half]
        part[now, 1, rr, :, at] = acc[half:]

    for t in range(SLOTS - 1):
        b_copy(jnp.int32(t)).start()

    barrier = pltpu.get_barrier_semaphore()

    @pl.loop(1, cols)
    def _(k):
        pl.semaphore_signal(
            barrier, inc=1, device_id={"col": lax.rem(c + k, cols)}, device_id_type=MESH
        )

    @pl.loop(1, rows)
    def _(k):
        pl.semaphore_signal(
            barrier, inc=1, device_id={"row": lax.rem(r + k, rows)}, device_id_type=MESH
        )

    pl.semaphore_wait(barrier, cols - 1 + rows - 1)

    @pl.loop(1, cols)
    def _(k):
        a_copy(0, k, c).start()

    own_copy(0).start()

    @pl.loop(0, chunks)
    def _(s):
        @pl.loop(1, cols)
        def _(k):
            a_copy(s, k, c).wait_send()

            @pl.when(s + 1 < chunks)
            def _():
                a_copy(s + 1, k, c).start()

        own_copy(s).wait()

        @pl.when(s + 1 < chunks)
        def _():
            own_copy(s + 1).start()

        @pl.loop(1, cols)
        def _(k):
            a_copy(s, k, lax.rem(c - k + cols, cols)).wait_recv()

        @pl.loop(0, depth // kt)
        def _(kk):
            at = pl.ds(pl.multiple_of(kk * kt, 128), kt)
            block = recv[s, :, at]
            high = block.astype(BF16)
            xhi[:, at] = high
            xlo[:, at] = (block - high.astype(F32)).astype(BF16)

        @pl.loop(0, rows)
        def _(jr):
            @pl.loop(0, per)
            def _(jt):
                tile(s, jr, jt)

            pair_copy(s, jr).start()

            @pl.when(jr > 0)
            def _():
                pair_finish(s, jr - 1)
                z_copy(s, jr - 1).start()

        pair_finish(s, rows - 1)

        @pl.when(s > 0)
        def _():
            z_finish(s - 1)

        @pl.when(s > 1)
        def _():
            plane_finish(s - 2)

    z_finish(chunks - 1)
    plane_finish(chunks - 2)
    plane_finish(chunks - 1)


def body(rows, cols, amplitudes, integrals):
    occupied = amplitudes.shape[0]
    depth, width = integrals.shape
    m = max(8, occupied // CHUNKS)
    chunks = occupied // m
    slab = width // rows
    tn = 256 if slab % 256 == 0 else 128
    kt = min(512, depth)
    chips = cols // 2
    half = chips * m
    dma = pltpu.SemaphoreType.DMA
    vmem = pltpu.VMEM
    return pl.pallas_call(
        functools.partial(kernel, rows, cols, m, chunks, depth, tn, kt),
        out_shape=jax.ShapeDtypeStruct((occupied, slab), F32),
        in_specs=[pl.BlockSpec(memory_space=pl.ANY)] * 2,
        out_specs=pl.BlockSpec(memory_space=vmem),
        scratch_shapes=[
            vmem((chunks, cols * m, depth), F32),
            vmem((cols * m, depth), BF16),
            vmem((cols * m, depth), BF16),
            vmem((SLOTS, depth, tn), F32),
            vmem((cols * m, tn), F32),
            vmem((2, 2, rows, half, slab), F32),
            vmem((chunks, rows, half, slab), F32),
            vmem((chunks, rows - 1, half, slab), F32),
            vmem((chunks, half, slab), F32),
            vmem((chunks, chips - 1, m, slab), F32),
            dma((chunks,)),
            dma((chunks, cols - 1)),
            dma((chunks, cols - 1)),
            dma((SLOTS,)),
            dma((chunks, rows)),
            dma((chunks, rows)),
            dma((chunks, rows - 1)),
            dma((chunks, rows - 1)),
            dma((chunks, chips - 1)),
            dma((chunks, chips - 1)),
        ],
        compiler_params=pltpu.CompilerParams(
            collective_id=0, has_side_effects=True, vmem_limit_bytes=60 * 2**20
        ),
        cost_estimate=pl.CostEstimate(
            flops=6 * occupied * cols * depth * width,
            bytes_accessed=4 * chunks * depth * width,
            transcendentals=0,
        ),
        name="ladder_exchange",
    )(amplitudes, integrals)


def solution(mesh):
    rows, cols = mesh.shape["row"], mesh.shape["col"]
    return jax.shard_map(
        functools.partial(body, rows, cols),
        mesh=mesh,
        in_specs=(P("col", "row"), P(("row", "col"), None)),
        out_specs=P("col", "row"),
        check_vma=False,
    )
```

```python
import functools

import jax
import jax.numpy as jnp
from jax import lax
from jax.experimental import pallas as pl
from jax.experimental.pallas import tpu as pltpu
from jax.sharding import PartitionSpec as P

MESH = pl.DeviceIdType.MESH
BF16, F32 = jnp.bfloat16, jnp.float32
SLOTS = 5
CHUNKS = 8


def kernel(
    rows, cols, m, chunks, depth, tn, kt,
    a, b, out,
    recv, x, bbuf, acc, part, pair_in, z_in, plane, plane_in,
    own_sem, a_send, a_recv, b_sem, p_send, p_recv, z_send, z_recv, q_send, q_recv,
):
    r, c = lax.axis_index("row"), lax.axis_index("col")
    chips = cols // 2
    core, chip = lax.rem(c, 2), lax.div(c, 2)
    sibling = c + 1 - 2 * core
    half, wide = chips * m, cols * m
    slab = out.shape[1]
    per = slab // tn
    tiles = rows * per

    def place(col):
        return pl.multiple_of((lax.rem(col, 2) * chips + lax.div(col, 2)) * m, 8)

    def own_copy(s):
        return pltpu.make_async_copy(
            a.at[pl.ds(pl.multiple_of(s * m, 8), m), pl.ds(pl.multiple_of(c * depth, 128), depth)],
            recv.at[s, pl.ds(place(c), m)],
            own_sem.at[s],
        )

    def a_copy(s, k, slot_of):
        peer = lax.rem(c + k, cols)
        return pltpu.make_async_remote_copy(
            src_ref=a.at[
                pl.ds(pl.multiple_of(s * m, 8), m), pl.ds(pl.multiple_of(peer * depth, 128), depth)
            ],
            dst_ref=recv.at[s, pl.ds(place(slot_of), m)],
            send_sem=a_send.at[s, k - 1],
            recv_sem=a_recv.at[s, k - 1],
            device_id={"col": peer},
            device_id_type=MESH,
        )

    def b_copy(t):
        j = lax.rem(t, tiles)
        rr = lax.rem(r + 1 + lax.div(j, per), rows)
        col = rr * slab + lax.rem(j, per) * tn
        return pltpu.make_async_copy(
            b.at[:, pl.ds(pl.multiple_of(col, 128), tn)],
            bbuf.at[lax.rem(t, SLOTS)],
            b_sem.at[lax.rem(t, SLOTS)],
        )

    def pair_copy(s, jr):
        rr = lax.rem(r + 1 + jr, rows)
        return pltpu.make_async_remote_copy(
            src_ref=part.at[lax.rem(s, 2), 1 - core, rr],
            dst_ref=pair_in.at[s, jr],
            send_sem=p_send.at[s, jr],
            recv_sem=p_recv.at[s, jr],
            device_id={"col": sibling},
            device_id_type=MESH,
        )

    def z_copy(s, jr):
        rr = lax.rem(r + 1 + jr, rows)
        return pltpu.make_async_remote_copy(
            src_ref=part.at[lax.rem(s, 2), core, rr],
            dst_ref=z_in.at[s, jr],
            send_sem=z_send.at[s, jr],
            recv_sem=z_recv.at[s, jr],
            device_id={"row": rr},
            device_id_type=MESH,
        )

    def plane_copy(s, k):
        there = lax.rem(chip + k, chips)
        return pltpu.make_async_remote_copy(
            src_ref=plane.at[s, pl.ds(pl.multiple_of(there * m, 8), m)],
            dst_ref=plane_in.at[s, k - 1],
            send_sem=q_send.at[s, k - 1],
            recv_sem=q_recv.at[s, k - 1],
            device_id={"col": 2 * there + core},
            device_id_type=MESH,
        )

    def pair_finish(s, jr):
        rr = lax.rem(r + 1 + jr, rows)
        copy = pair_copy(s, jr)
        copy.wait_recv()
        copy.wait_send()
        now = lax.rem(s, 2)
        part[now, core, rr] = part[now, core, rr] + pair_in[s, jr]

    def z_finish(s):
        @pl.loop(0, rows - 1)
        def _(k):
            copy = z_copy(s, k)
            copy.wait_recv()
            copy.wait_send()

        total = part[lax.rem(s, 2), core, r]
        for k in range(rows - 1):
            total = total + z_in[s, k]
        plane[s] = total

        @pl.loop(1, chips)
        def _(k):
            plane_copy(s, k).start()

    def plane_finish(s):
        @pl.loop(1, chips)
        def _(k):
            copy = plane_copy(s, k)
            copy.wait_recv()
            copy.wait_send()

        total = plane[s, pl.ds(pl.multiple_of(chip * m, 8), m)]
        for k in range(chips - 1):
            total = total + plane_in[s, k]
        out[pl.ds(pl.multiple_of(s * m, 8), m), :] = 0.5 * total

    def tile(s, jr, jt):
        rr = lax.rem(r + 1 + jr, rows)
        t = s * tiles + jr * per + jt
        b_copy(t).wait()

        @pl.when(t + SLOTS - 1 < chunks * tiles)
        def _():
            b_copy(t + SLOTS - 1).start()

        slot = lax.rem(t, SLOTS)
        acc[...] = jnp.zeros_like(acc)

        @pl.loop(0, depth // kt)
        def _(kk):
            at = pl.ds(pl.multiple_of(kk * kt, 128), kt)
            block = bbuf[slot, at, :]
            bh = block.astype(BF16)
            bl = (block - bh.astype(F32)).astype(BF16)
            both = jnp.dot(x[:, at], bh, preferred_element_type=F32)
            acc[...] += (
                both[:wide] + both[wide:]
                + jnp.dot(x[:wide, at], bl, preferred_element_type=F32)
            )

        now = lax.rem(s, 2)
        at = pl.ds(pl.multiple_of(jt * tn, 128), tn)
        part[now, 0, rr, :, at] = acc[:half]
        part[now, 1, rr, :, at] = acc[half:]

    for t in range(SLOTS - 1):
        b_copy(jnp.int32(t)).start()

    barrier = pltpu.get_barrier_semaphore()

    @pl.loop(1, cols)
    def _(k):
        pl.semaphore_signal(
            barrier, inc=1, device_id={"col": lax.rem(c + k, cols)}, device_id_type=MESH
        )

    @pl.loop(1, rows)
    def _(k):
        pl.semaphore_signal(
            barrier, inc=1, device_id={"row": lax.rem(r + k, rows)}, device_id_type=MESH
        )

    pl.semaphore_wait(barrier, cols - 1 + rows - 1)

    @pl.loop(1, cols)
    def _(k):
        a_copy(0, k, c).start()

    own_copy(0).start()

    @pl.loop(0, chunks)
    def _(s):
        @pl.loop(1, cols)
        def _(k):
            a_copy(s, k, c).wait_send()

            @pl.when(s + 1 < chunks)
            def _():
                a_copy(s + 1, k, c).start()

        own_copy(s).wait()

        @pl.when(s + 1 < chunks)
        def _():
            own_copy(s + 1).start()

        @pl.loop(1, cols)
        def _(k):
            a_copy(s, k, lax.rem(c - k + cols, cols)).wait_recv()

        @pl.loop(0, depth // kt)
        def _(kk):
            at = pl.ds(pl.multiple_of(kk * kt, 128), kt)
            block = recv[s, :, at]
            high = block.astype(BF16)
            x[:wide, at] = high
            x[wide:, at] = (block - high.astype(F32)).astype(BF16)

        @pl.loop(0, rows)
        def _(jr):
            @pl.loop(0, per)
            def _(jt):
                tile(s, jr, jt)

            pair_copy(s, jr).start()

            @pl.when(jr > 0)
            def _():
                pair_finish(s, jr - 1)
                z_copy(s, jr - 1).start()

        pair_finish(s, rows - 1)

        @pl.when(s > 0)
        def _():
            z_finish(s - 1)

        @pl.when(s > 1)
        def _():
            plane_finish(s - 2)

    z_finish(chunks - 1)
    plane_finish(chunks - 2)
    plane_finish(chunks - 1)


def body(rows, cols, amplitudes, integrals):
    occupied = amplitudes.shape[0]
    depth, width = integrals.shape
    m = max(8, occupied // CHUNKS)
    chunks = occupied // m
    slab = width // rows
    tn = 256 if slab % 256 == 0 else 128
    kt = min(1024, depth)
    chips = cols // 2
    half = chips * m
    dma = pltpu.SemaphoreType.DMA
    vmem = pltpu.VMEM
    return pl.pallas_call(
        functools.partial(kernel, rows, cols, m, chunks, depth, tn, kt),
        out_shape=jax.ShapeDtypeStruct((occupied, slab), F32),
        in_specs=[pl.BlockSpec(memory_space=pl.ANY)] * 2,
        out_specs=pl.BlockSpec(memory_space=vmem),
        scratch_shapes=[
            vmem((chunks, cols * m, depth), F32),
            vmem((2 * cols * m, depth), BF16),
            vmem((SLOTS, depth, tn), F32),
            vmem((cols * m, tn), F32),
            vmem((2, 2, rows, half, slab), F32),
            vmem((chunks, rows, half, slab), F32),
            vmem((chunks, rows - 1, half, slab), F32),
            vmem((chunks, half, slab), F32),
            vmem((chunks, chips - 1, m, slab), F32),
            dma((chunks,)),
            dma((chunks, cols - 1)),
            dma((chunks, cols - 1)),
            dma((SLOTS,)),
            dma((chunks, rows)),
            dma((chunks, rows)),
            dma((chunks, rows - 1)),
            dma((chunks, rows - 1)),
            dma((chunks, chips - 1)),
            dma((chunks, chips - 1)),
        ],
        compiler_params=pltpu.CompilerParams(
            collective_id=0, has_side_effects=True, vmem_limit_bytes=60 * 2**20
        ),
        cost_estimate=pl.CostEstimate(
            flops=6 * occupied * cols * depth * width,
            bytes_accessed=4 * chunks * depth * width,
            transcendentals=0,
        ),
        name="ladder_exchange",
    )(amplitudes, integrals)


def solution(mesh):
    rows, cols = mesh.shape["row"], mesh.shape["col"]
    return jax.shard_map(
        functools.partial(body, rows, cols),
        mesh=mesh,
        in_specs=(P("col", "row"), P(("row", "col"), None)),
        out_specs=P("col", "row"),
        check_vma=False,
    )
```

```python
import functools

import jax
import jax.numpy as jnp
from jax import lax
from jax.experimental import pallas as pl
from jax.experimental.pallas import tpu as pltpu
from jax.sharding import PartitionSpec as P

MESH = pl.DeviceIdType.MESH
BF16, F32 = jnp.bfloat16, jnp.float32
SLOTS = 5
CHUNKS = 8


def kernel(
    rows, cols, m, chunks, depth, tn, kt,
    a, b, out,
    recv, x, bbuf, acc, part, pair_in, z_in, plane, plane_in,
    own_sem, a_send, a_recv, b_sem, p_send, p_recv, z_send, z_recv, q_send, q_recv,
):
    r, c = lax.axis_index("row"), lax.axis_index("col")
    chips = cols // 2
    core, chip = lax.rem(c, 2), lax.div(c, 2)
    sibling = c + 1 - 2 * core
    half, wide = chips * m, cols * m
    slab = out.shape[1]
    per = slab // tn
    tiles = rows * per

    def place(col):
        return pl.multiple_of((lax.rem(col, 2) * chips + lax.div(col, 2)) * m, 8)

    def own_copy(s):
        return pltpu.make_async_copy(
            a.at[pl.ds(pl.multiple_of(s * m, 8), m), pl.ds(pl.multiple_of(c * depth, 128), depth)],
            recv.at[s, pl.ds(place(c), m)],
            own_sem.at[s],
        )

    def a_copy(s, k, slot_of):
        peer = lax.rem(c + k, cols)
        return pltpu.make_async_remote_copy(
            src_ref=a.at[
                pl.ds(pl.multiple_of(s * m, 8), m), pl.ds(pl.multiple_of(peer * depth, 128), depth)
            ],
            dst_ref=recv.at[s, pl.ds(place(slot_of), m)],
            send_sem=a_send.at[s, k - 1],
            recv_sem=a_recv.at[s, k - 1],
            device_id={"col": peer},
            device_id_type=MESH,
        )

    def b_copy(t):
        j = lax.rem(t, tiles)
        rr = lax.rem(r + 1 + lax.div(j, per), rows)
        col = rr * slab + lax.rem(j, per) * tn
        return pltpu.make_async_copy(
            b.at[:, pl.ds(pl.multiple_of(col, 128), tn)],
            bbuf.at[lax.rem(t, SLOTS)],
            b_sem.at[lax.rem(t, SLOTS)],
        )

    def pair_copy(s, jr):
        rr = lax.rem(r + 1 + jr, rows)
        return pltpu.make_async_remote_copy(
            src_ref=part.at[lax.rem(s, 2), 1 - core, rr],
            dst_ref=pair_in.at[s, jr],
            send_sem=p_send.at[s, jr],
            recv_sem=p_recv.at[s, jr],
            device_id={"col": sibling},
            device_id_type=MESH,
        )

    def z_copy(s, jr):
        rr = lax.rem(r + 1 + jr, rows)
        return pltpu.make_async_remote_copy(
            src_ref=part.at[lax.rem(s, 2), core, rr],
            dst_ref=z_in.at[s, jr],
            send_sem=z_send.at[s, jr],
            recv_sem=z_recv.at[s, jr],
            device_id={"row": rr},
            device_id_type=MESH,
        )

    def plane_copy(s, k):
        there = lax.rem(chip + k, chips)
        return pltpu.make_async_remote_copy(
            src_ref=plane.at[s, pl.ds(pl.multiple_of(there * m, 8), m)],
            dst_ref=plane_in.at[s, k - 1],
            send_sem=q_send.at[s, k - 1],
            recv_sem=q_recv.at[s, k - 1],
            device_id={"col": 2 * there + core},
            device_id_type=MESH,
        )

    def pair_finish(s, jr):
        rr = lax.rem(r + 1 + jr, rows)
        copy = pair_copy(s, jr)
        copy.wait_recv()
        copy.wait_send()
        now = lax.rem(s, 2)
        part[now, core, rr] = part[now, core, rr] + pair_in[s, jr]

    def z_finish(s):
        @pl.loop(0, rows - 1)
        def _(k):
            copy = z_copy(s, k)
            copy.wait_recv()
            copy.wait_send()

        total = part[lax.rem(s, 2), core, r]
        for k in range(rows - 1):
            total = total + z_in[s, k]
        plane[s] = total

        @pl.loop(1, chips)
        def _(k):
            plane_copy(s, k).start()

    def plane_finish(s):
        @pl.loop(1, chips)
        def _(k):
            copy = plane_copy(s, k)
            copy.wait_recv()
            copy.wait_send()

        total = plane[s, pl.ds(pl.multiple_of(chip * m, 8), m)]
        for k in range(chips - 1):
            total = total + plane_in[s, k]
        out[pl.ds(pl.multiple_of(s * m, 8), m), :] = 0.5 * total

    def tile(s, jr, jt):
        rr = lax.rem(r + 1 + jr, rows)
        t = s * tiles + jr * per + jt
        b_copy(t).wait()

        @pl.when(t + SLOTS - 1 < chunks * tiles)
        def _():
            b_copy(t + SLOTS - 1).start()

        slot = lax.rem(t, SLOTS)
        acc[...] = jnp.zeros_like(acc)

        @pl.loop(0, depth // kt)
        def _(kk):
            at = pl.ds(pl.multiple_of(kk * kt, 128), kt)
            block = bbuf[slot, at, :]
            bh = block.astype(BF16)
            bl = (block - bh.astype(F32)).astype(BF16)
            both = jnp.dot(x[:, at], bh, preferred_element_type=F32)
            acc[...] += (
                both[:wide] + both[wide:]
                + jnp.dot(x[:wide, at], bl, preferred_element_type=F32)
            )

        now = lax.rem(s, 2)
        at = pl.ds(pl.multiple_of(jt * tn, 128), tn)
        part[now, 0, rr, :, at] = acc[:half]
        part[now, 1, rr, :, at] = acc[half:]

    for t in range(SLOTS - 1):
        b_copy(jnp.int32(t)).start()

    barrier = pltpu.get_barrier_semaphore()

    @pl.loop(1, cols)
    def _(k):
        pl.semaphore_signal(
            barrier, inc=1, device_id={"col": lax.rem(c + k, cols)}, device_id_type=MESH
        )

    @pl.loop(1, rows)
    def _(k):
        pl.semaphore_signal(
            barrier, inc=1, device_id={"row": lax.rem(r + k, rows)}, device_id_type=MESH
        )

    pl.semaphore_wait(barrier, cols - 1 + rows - 1)

    @pl.loop(1, cols)
    def _(k):
        a_copy(0, k, c).start()

    own_copy(0).start()

    @pl.loop(0, chunks)
    def _(s):
        @pl.loop(1, cols)
        def _(k):
            a_copy(s, k, c).wait_send()

            @pl.when(s + 1 < chunks)
            def _():
                a_copy(s + 1, k, c).start()

        own_copy(s).wait()

        @pl.when(s + 1 < chunks)
        def _():
            own_copy(s + 1).start()

        @pl.loop(1, cols)
        def _(k):
            a_copy(s, k, lax.rem(c - k + cols, cols)).wait_recv()

        @pl.loop(0, depth // kt)
        def _(kk):
            at = pl.ds(pl.multiple_of(kk * kt, 128), kt)
            block = recv[s, :, at]
            high = block.astype(BF16)
            x[:wide, at] = high
            x[wide:, at] = (block - high.astype(F32)).astype(BF16)

        @pl.loop(0, rows)
        def _(jr):
            @pl.loop(0, per)
            def _(jt):
                tile(s, jr, jt)

            pair_copy(s, jr).start()

            @pl.when(jr > 0)
            def _():
                pair_finish(s, jr - 1)
                z_copy(s, jr - 1).start()

        pair_finish(s, rows - 1)

        @pl.when(s > 0)
        def _():
            z_finish(s - 1)

        @pl.when(s > 1)
        def _():
            plane_finish(s - 2)

    z_finish(chunks - 1)
    plane_finish(chunks - 2)
    plane_finish(chunks - 1)


def body(rows, cols, amplitudes, integrals):
    occupied = amplitudes.shape[0]
    depth, width = integrals.shape
    m = max(8, occupied // CHUNKS)
    chunks = occupied // m
    slab = width // rows
    tn = 256 if slab % 256 == 0 else 128
    kt = min(2048, depth)
    chips = cols // 2
    half = chips * m
    dma = pltpu.SemaphoreType.DMA
    vmem = pltpu.VMEM
    return pl.pallas_call(
        functools.partial(kernel, rows, cols, m, chunks, depth, tn, kt),
        out_shape=jax.ShapeDtypeStruct((occupied, slab), F32),
        in_specs=[pl.BlockSpec(memory_space=pl.ANY)] * 2,
        out_specs=pl.BlockSpec(memory_space=vmem),
        scratch_shapes=[
            vmem((chunks, cols * m, depth), F32),
            vmem((2 * cols * m, depth), BF16),
            vmem((SLOTS, depth, tn), F32),
            vmem((cols * m, tn), F32),
            vmem((2, 2, rows, half, slab), F32),
            vmem((chunks, rows, half, slab), F32),
            vmem((chunks, rows - 1, half, slab), F32),
            vmem((chunks, half, slab), F32),
            vmem((chunks, chips - 1, m, slab), F32),
            dma((chunks,)),
            dma((chunks, cols - 1)),
            dma((chunks, cols - 1)),
            dma((SLOTS,)),
            dma((chunks, rows)),
            dma((chunks, rows)),
            dma((chunks, rows - 1)),
            dma((chunks, rows - 1)),
            dma((chunks, chips - 1)),
            dma((chunks, chips - 1)),
        ],
        compiler_params=pltpu.CompilerParams(
            collective_id=0, has_side_effects=True, vmem_limit_bytes=60 * 2**20
        ),
        cost_estimate=pl.CostEstimate(
            flops=6 * occupied * cols * depth * width,
            bytes_accessed=4 * chunks * depth * width,
            transcendentals=0,
        ),
        name="ladder_exchange",
    )(amplitudes, integrals)


def solution(mesh):
    rows, cols = mesh.shape["row"], mesh.shape["col"]
    return jax.shard_map(
        functools.partial(body, rows, cols),
        mesh=mesh,
        in_specs=(P("col", "row"), P(("row", "col"), None)),
        out_specs=P("col", "row"),
        check_vma=False,
    )
```
